256 devices in a mesh: gx: 32 (over y, x, core), gy: 8 (over z).
Axes of the slice: x: 4, y: 4, z: 8, core: 2. Of those that a mesh axis runs over, the one named last changes fastest.
Arguments:
- edge_embed: bfloat16 [524288, 512], P(('gx', 'gy')), may hold values from -6 to 6
- cotangent: bfloat16 [524288, 512], P(('gx', 'gy')), may hold values from -6 to 6
- w_down: bfloat16 [512, 64], replicated, may hold values from -0.25 to 0.25
- w_bilinear: bfloat16 [512, 64], replicated, may hold values from -0.25 to 0.25
- w_up: bfloat16 [64, 512], replicated, may hold values from -0.75 to 0.75
- in_index: int32 [2304, 768], P(('gx', 'gy')), may hold values from 0 to 2047
- out_index: int32 [2304, 768], P(('gx', 'gy')), may hold values from 0 to 2047
- triplet_cos: float32 [2304, 768], P(('gx', 'gy')), may hold values from -1 to 1
- block_counts: int32 [2304, 12], P(('gx', 'gy')), may hold values from 1 to 64, as said below
Outputs:
- updated: bfloat16 [524288, 512], P(('gx', 'gy'))
- grad_embed: bfloat16 [524288, 512], P(('gx', 'gy'))
- grad_down: float32 [512, 64], replicated
- grad_bilinear: float32 [512, 64], replicated
- grad_up: float32 [64, 512], replicated
The draws below stay inside these ranges and needn't reach their ends.
Inputs may be any that keep to these rules, and one draw needn't show every extreme that they name: `block_counts`: each group of nine rows (one grid block) has at least one entry equal to 64; loads differ from block to block.
All inputs are finite; a program needn't handle non-finite values.
Results may differ from the reference program's by a relative error of at most 0.007.
Values may be sent and summed in bfloat16 or wider, within the bound.
No kernel may reach another device: no remote copies, remote signals or barrier semaphores. Data moves between devices by JAX's collectives and lax.ppermute only.
A program may use at most 128 MiB of HBM per device.

```python
import jax
import jax.numpy as jnp
from jax import lax

D = 512
DT = 64
L = 8
TB = 64
E_DEV = 2048
NB = 12
SLOTS = 768
EDGES = 524288
BLOCKS_ALL = 2304
N_GX = 32
N_GY = 8
DEVICES = 256


def draw_block_counts(key, part):
    key = jax.random.fold_in(key, 11)
    key_level, key_raw, key_pair, key_block = jax.random.split(key, 4)
    level = jax.random.randint(key_level, (DEVICES, 1, 1), 1, 5)
    raw = jax.random.randint(key_raw, (DEVICES, 9, NB), 1, TB + 1)
    counts = 1 + (raw - 1) * level // 4
    full_pair = jax.random.randint(key_pair, (DEVICES, 1, 1), 0, 9)
    full_block = jax.random.randint(key_block, (DEVICES, 1, 1), 0, NB)
    pair_ids = jnp.arange(9, dtype=jnp.int32)[None, :, None]
    block_ids = jnp.arange(NB, dtype=jnp.int32)[None, None, :]
    chosen = (pair_ids == full_pair) & (block_ids == full_block)
    counts = jnp.where(chosen, TB, counts)
    return counts.reshape(DEVICES * 9, NB).astype(jnp.int32)


def with_ends(result, stream_key, smallest, largest):
    index_at = [jax.random.randint(jax.random.fold_in(stream_key, axis), (), 0, length) for axis, length in enumerate(result.shape)]
    widest = result.shape.index(max(result.shape))
    beside = index_at[:widest] + [(index_at[widest] + 1) % result.shape[widest]] + index_at[widest + 1:]
    return result.at[tuple(index_at)].set(smallest).at[tuple(beside)].set(largest)


def block_levels(key, dims, cuts, smallest, largest):
    factor_of, own = 1.0, jax.random.fold_in(key, 6)
    for dim, blocks in cuts:
        draws = jnp.exp(jax.random.uniform(jax.random.fold_in(own, dim), (blocks,), jnp.float32, smallest / len(cuts), largest / len(cuts)))
        factor_of = factor_of * jnp.repeat(draws, dims[dim] // blocks).reshape([-1 if axis == dim else 1 for axis in range(len(dims))])
    return factor_of


def bell_draw(rng, extent, deviation, limit, cuts=(), kind=jnp.bfloat16):
    result = deviation * jax.random.normal(rng, extent, jnp.float32)
    if cuts:
        result = result * block_levels(rng, extent, cuts, -0.22, 0.18)
    return jnp.clip(result, -limit, limit).astype(kind)


def setup_inputs(seed: int = 0) -> dict:
    key_list = jax.random.split(jax.random.key(seed), 10)
    return {
        "edge_embed": bell_draw(key_list[0], (EDGES, D), 1.0, 6.0, ((0, 256),)),
        "cotangent": bell_draw(key_list[1], (EDGES, D), 1.0, 6.0, ((0, 256),)),
        "w_down": bell_draw(key_list[2], (D, DT), D ** -0.5, 0.25),
        "w_bilinear": bell_draw(key_list[3], (L * DT, DT), (L * DT) ** -0.5, 0.25),
        "w_up": bell_draw(key_list[4], (DT, D), DT ** -0.5, 0.75),
        "in_index": with_ends(jax.random.randint(key_list[5], (BLOCKS_ALL, SLOTS), 0, E_DEV), jax.random.fold_in(key_list[5], 1), 0, E_DEV - 1).astype(jnp.int32),
        "out_index": with_ends(jax.random.randint(key_list[6], (BLOCKS_ALL, SLOTS), 0, E_DEV), jax.random.fold_in(key_list[6], 1), 0, E_DEV - 1).astype(jnp.int32),
        "triplet_cos": jnp.clip(jax.random.uniform(key_list[7], (BLOCKS_ALL, SLOTS), jnp.float32, -1.0, 1.0) * block_levels(key_list[7], (BLOCKS_ALL, SLOTS), ((0, 256),), -0.4, 0.0), -1.0, 1.0),
        "block_counts": draw_block_counts(jax.random.fold_in(key_list[9], 71), 0),
    }


def legendre(cosine):
    terms = [jnp.ones_like(cosine), cosine]
    for order in range(1, L - 1):
        terms.append(((2 * order + 1) * cosine * terms[order] - order * terms[order - 1]) / (order + 1))
    return jnp.stack(terms[:L], axis=-1)

def silu_grad(value):
    sig = jax.nn.sigmoid(value)
    return sig * (1.0 + value * (1.0 - sig))

def slot_mask(counts):
    position = jnp.arange(SLOTS, dtype=jnp.int32) % TB
    return (position < jnp.repeat(counts, TB, total_repeat_length=SLOTS)).astype(jnp.float32)

def lift(source, in_idx, cosine):
    feat = jnp.take(source, in_idx, axis=0).astype(jnp.float32)
    basis = legendre(cosine)
    lifted = (basis[:, :, None] * feat[:, None, :]).astype(jnp.bfloat16)
    return (lifted.reshape(SLOTS, -1), basis)

def pair_forward(source, in_idx, out_idx, cosine, counts, w_bil):
    lifted, basis = lift(source, in_idx, cosine)
    message = jnp.dot(lifted, w_bil, preferred_element_type=jnp.float32) * slot_mask(counts)[:, None]
    return jax.ops.segment_sum(message, out_idx, num_segments=source.shape[0])

def pair_backward(source, in_idx, out_idx, cosine, counts, w_bil, d_trip):
    lifted, basis = lift(source, in_idx, cosine)
    valid = slot_mask(counts).astype(jnp.bfloat16)
    d_message = jnp.take(d_trip, out_idx, axis=0) * valid[:, None]
    grad_bil = jnp.dot(lifted.T, d_message, preferred_element_type=jnp.float32)
    d_lifted = jnp.dot(d_message, w_bil.T, preferred_element_type=jnp.float32)
    d_lifted = d_lifted.reshape(SLOTS, basis.shape[1], -1)
    d_feat = lax.optimization_barrier(jnp.sum(basis[:, :, None] * d_lifted, axis=1))
    d_source = jax.ops.segment_sum(d_feat, in_idx, num_segments=source.shape[0])
    return (d_source, grad_bil)

def reference(edge_embed, cotangent, w_down, w_bilinear, w_up, in_index, out_index, triplet_cos, block_counts):
    grid_x = N_GX
    grid_y = N_GY
    devs = grid_x * grid_y
    width_t = w_down.shape[1]
    pre_down = jnp.dot(edge_embed, w_down, preferred_element_type=jnp.float32)
    down = jax.nn.silu(pre_down).astype(jnp.bfloat16)
    down_grid = down.reshape(grid_x, grid_y, E_DEV, width_t)
    in_all = in_index.reshape(devs, 9, SLOTS)
    out_all = out_index.reshape(devs, 9, SLOTS)
    cos_all = triplet_cos.reshape(devs, 9, SLOTS)
    cnt_all = block_counts.reshape(devs, 9, -1)
    trip = jnp.zeros((devs, E_DEV, width_t), jnp.float32)
    for pair in range(9):
        row_off, col_off = divmod(pair, 3)
        source = jnp.roll(down_grid, (1 - row_off, 1 - col_off), axis=(0, 1)).reshape(devs, E_DEV, width_t)
        contrib = lax.map(lambda item: pair_forward(item[0], item[1], item[2], item[3], item[4], w_bilinear), (source, in_all[:, pair], out_all[:, pair], cos_all[:, pair], cnt_all[:, pair]))
        trip = trip + contrib
    trip_b = trip.reshape(-1, width_t).astype(jnp.bfloat16)
    up_act = jnp.dot(trip_b, w_up, preferred_element_type=jnp.float32)
    updated = (edge_embed.astype(jnp.float32) + jax.nn.silu(up_act)).astype(jnp.bfloat16)
    cot_f = cotangent.astype(jnp.float32)
    d_act = (cot_f * silu_grad(up_act)).astype(jnp.bfloat16)
    grad_up = jnp.dot(trip_b.T, d_act, preferred_element_type=jnp.float32)
    d_trip = jnp.dot(d_act, w_up.T, preferred_element_type=jnp.float32).astype(jnp.bfloat16)
    d_trip_all = d_trip.reshape(devs, E_DEV, width_t)
    d_down = jnp.zeros((grid_x, grid_y, E_DEV, width_t), jnp.float32)
    grad_bil = jnp.zeros(w_bilinear.shape, jnp.float32)
    for pair in range(9):
        row_off, col_off = divmod(pair, 3)
        source = jnp.roll(down_grid, (1 - row_off, 1 - col_off), axis=(0, 1)).reshape(devs, E_DEV, width_t)
        d_source, g_bil = lax.map(lambda item: pair_backward(item[0], item[1], item[2], item[3], item[4], w_bilinear, item[5]), (source, in_all[:, pair], out_all[:, pair], cos_all[:, pair], cnt_all[:, pair], d_trip_all))
        grad_bil = grad_bil + lax.optimization_barrier(jnp.sum(g_bil, axis=0))
        d_down = d_down + jnp.roll(d_source.reshape(grid_x, grid_y, E_DEV, width_t), (row_off - 1, col_off - 1), axis=(0, 1))
    d_pre = (d_down.reshape(-1, width_t) * silu_grad(pre_down)).astype(jnp.bfloat16)
    grad_down = jnp.dot(edge_embed.T, d_pre, preferred_element_type=jnp.float32)
    grad_embed = (cot_f + jnp.dot(d_pre, w_down.T, preferred_element_type=jnp.float32)).astype(jnp.bfloat16)
    scale = float(EDGES) ** (-0.5)
    return (updated, grad_embed, grad_down * scale, grad_bil * scale, grad_up * scale)
```

```python
import functools

import jax
import jax.numpy as jnp
from jax import lax
from jax.experimental import pallas as pl
from jax.experimental.pallas import tpu as pltpu
from jax.sharding import PartitionSpec as P

L = 8
DT = 64
TB = 64
SLOTS = 768
Q = 256
F32 = jnp.float32
BF16 = jnp.bfloat16
VMEM_LIMIT = 48 * 2**20

NN = (((1,), (0,)), ((), ()))
NT = (((1,), (1,)), ((), ()))
TN = (((0,), (0,)), ((), ()))


def dot(a, b, dims):
    return lax.dot_general(a, b, dims, preferred_element_type=F32)


def sigmoid(value):
    return 0.5 * jnp.tanh(0.5 * value) + 0.5


def legendre(cosine):
    terms = [jnp.ones_like(cosine), cosine]
    for order in range(1, L - 1):
        terms.append(
            ((2 * order + 1) * cosine * terms[order] - order * terms[order - 1])
            * (1.0 / (order + 1))
        )
    return terms


def valid_row(counts_ref, k):
    lane = lax.broadcasted_iota(jnp.int32, (1, 2 * TB), 1)
    rows = []
    for t in range(SLOTS // (2 * TB)):
        count = jnp.where(lane < TB, counts_ref[k, 2 * t], counts_ref[k, 2 * t + 1])
        rows.append(((lane & (TB - 1)) < count).astype(F32))
    return jnp.concatenate(rows, axis=1)


def one_hot(index):
    low = (index & (Q - 1)).astype(F32).astype(BF16)
    row = lax.broadcasted_iota(jnp.int32, (Q, 128), 0).astype(F32).astype(BF16)
    row = jnp.concatenate([row] * (SLOTS // 128), axis=1)
    return jnp.where(row == low, jnp.ones((), BF16), jnp.zeros((), BF16))


def stacked(table):
    parts = table.shape[1] // Q
    return jnp.concatenate([table[:, r * Q : (r + 1) * Q] for r in range(parts)], axis=0)


def pick(table, hot, high):
    parts = table.shape[1] // Q
    found = dot(stacked(table), hot, NN)
    total = found[:DT]
    for r in range(1, parts):
        total = jnp.where(high == r, found[r * DT : (r + 1) * DT], total)
    return total


def collect(values, hot, high, parts):
    low = values.astype(BF16)
    zero = jnp.zeros((), BF16)
    rows = [jnp.where(high == r, low, zero) for r in range(parts)]
    return dot(jnp.concatenate(rows, axis=0), hot, NT)


def expand(basis, values):
    return jnp.concatenate([(row * values).astype(BF16) for row in basis], axis=0)


def down_kernel(edge_ref, w_ref, down_ref, slope_ref):
    pre = dot(w_ref[...], edge_ref[...], (((0,), (1,)), ((), ())))
    sig = sigmoid(pre)
    down_ref[...] = (pre * sig).astype(BF16)
    slope_ref[...] = sig * (1.0 + pre * (1.0 - sig))


def forward_kernel(pairs, base, counts_ref, in_ref, out_ref, cos_ref, w_ref, *refs):
    n = len(pairs)
    sources = refs[:n]
    total_ref = refs[n] if base else None
    trip_ref, feat_ref = refs[-2:]
    w_t = w_ref[...].T
    parts = sources[0].shape[1] // Q
    for i, k in enumerate(pairs):
        in_idx = in_ref[k : k + 1, :]
        out_idx = out_ref[k : k + 1, :]
        feat = pick(sources[i][...], one_hot(in_idx), in_idx // Q)
        feat_ref[i * DT : (i + 1) * DT, :] = feat.astype(BF16)
        lifted = expand(legendre(cos_ref[k : k + 1, :]), feat)
        message = dot(w_t, lifted, NN) * valid_row(counts_ref, k)
        part = collect(message, one_hot(out_idx), out_idx // Q, parts)
        if i == 0:
            trip_ref[...] = part + total_ref[...] if base else part
        else:
            trip_ref[...] += part


def middle_kernel(edge_ref, cot_ref, trip_ref, w_ref, updated_ref, d_trip_ref, grad_ref):
    trip = trip_ref[...].astype(BF16)
    up_act = dot(trip, w_ref[...], TN)
    sig = sigmoid(up_act)
    silu = up_act * sig
    updated_ref[...] = (edge_ref[...].astype(F32) + silu).astype(BF16)
    slope = sig * (1.0 + up_act - silu)
    d_act = (cot_ref[...].astype(F32) * slope).astype(BF16)
    d_trip_ref[...] = dot(w_ref[...], d_act, NT).astype(BF16)
    part = dot(trip, d_act, NN)

    @pl.when(pl.program_id(0) == 0)
    def _():
        grad_ref[...] = part

    @pl.when(pl.program_id(0) > 0)
    def _():
        grad_ref[...] += part


def backward_kernel(pairs, base, counts_ref, in_ref, out_ref, cos_ref, w_ref, d_trip_ref, *refs):
    feat_refs = refs[: len(pairs)]
    grad_base = refs[len(pairs)] if base else None
    d_ref, grad_ref = refs[-2:]
    w = w_ref[...]
    w_rows = jnp.concatenate([w[l * DT : (l + 1) * DT] for l in range(L)], axis=1)
    d_trip = d_trip_ref[...]
    parts = d_trip.shape[1] // Q
    for i, k in enumerate(pairs):
        in_idx = in_ref[k : k + 1, :]
        out_idx = out_ref[k : k + 1, :]
        d_message = pick(d_trip, one_hot(out_idx), out_idx // Q) * valid_row(counts_ref, k)
        spread = expand(legendre(cos_ref[k : k + 1, :]), d_message)
        part = dot(feat_refs[i][...], spread, NT)
        if i == 0:
            grad_ref[...] = part + grad_base[...] if base else part
        else:
            grad_ref[...] += part
        d_feat = dot(w_rows, spread, NN)
        d_source = collect(d_feat, one_hot(in_idx), in_idx // Q, parts).astype(d_ref.dtype)
        for r in range(parts):
            d_ref[i, :, r * Q : (r + 1) * Q] = d_source[r * DT : (r + 1) * DT]


def final_kernel(edge_ref, slope_ref, *refs):
    terms = refs[:-2]
    d_pre_ref, grad_ref = refs[-2:]
    d_down = terms[0][...].astype(F32)
    for term in terms[1:]:
        d_down = d_down + term[...].astype(F32)
    d_pre = (d_down * slope_ref[...]).astype(BF16)
    d_pre_ref[...] = d_pre
    grad_ref[...] = dot(d_pre, edge_ref[...], NN)


def embed_kernel(cot_ref, d_pre_ref, w_ref, grad_ref):
    part = dot(d_pre_ref[...], w_ref[...], (((0,), (1,)), ((), ())))
    grad_ref[...] = (cot_ref[...].astype(F32) + part).astype(BF16)


def finish_kernel(scale, down_ref, bil_ref, up_ref, out_down, out_bil, out_up):
    out_down[...] = down_ref[...].T * scale
    for l in range(L):
        out_bil[l * DT : (l + 1) * DT, :] = bil_ref[:, l * DT : (l + 1) * DT] * scale
    out_up[...] = up_ref[...] * scale


def call(kernel, outs, args, us, smem=()):
    vmem = pl.BlockSpec(memory_space=pltpu.VMEM)
    scalar = pl.BlockSpec(memory_space=pltpu.SMEM)
    return pl.pallas_call(
        kernel,
        out_shape=outs,
        in_specs=[scalar if i in smem else vmem for i in range(len(args))],
        out_specs=jax.tree.map(lambda _: vmem, outs),
        compiler_params=pltpu.CompilerParams(vmem_limit_bytes=VMEM_LIMIT),
        cost_estimate=pl.CostEstimate(
            flops=int(us * 1.0e9), bytes_accessed=int(us * 3.0e6), transcendentals=0
        ),
    )(*args)


def shift(x, axis, step):
    n = lax.axis_size(axis)
    return lax.ppermute(x, axis, [(i, (i + step) % n) for i in range(n)])


def all_sum(x):
    nx, ny = lax.axis_size("gx"), lax.axis_size("gy")
    core = lax.rem(lax.axis_index("gx"), 2)
    half = x.shape[0] // 2

    def swap(value, axis, partner):
        n = lax.axis_size(axis)
        return lax.ppermute(value, axis, [(i, partner(i)) for i in range(n)])

    low, high = x[:half], x[half:]
    mine = jnp.where(core == 0, low, high)
    total = mine + swap(jnp.where(core == 0, high, low), "gx", lambda i: i ^ 1)
    side = 4
    steps = []
    for unit in (2, 2 * side):
        steps.append(("gx", lambda i, u=unit: i ^ u))
        steps.append(
            ("gx", lambda i, u=unit: i + (side - 1 - 2 * (i // u % side)) * u)
        )
    bit = 1
    while bit < ny:
        steps.append(("gy", lambda i, b=bit: i ^ b))
        bit *= 2
    for axis, partner in steps:
        total = total + swap(total, axis, partner)
    other = swap(total, "gx", lambda i: i ^ 1)
    first = jnp.where(core == 0, total, other)
    second = jnp.where(core == 0, other, total)
    return jnp.concatenate([first, second], axis=0)


def shards(
    edge_embed, cotangent, w_down, w_bilinear, w_up, in_index, out_index, triplet_cos, block_counts
):
    edges, width = edge_embed.shape
    struct = jax.ShapeDtypeStruct
    table = struct((DT, edges), BF16)
    stack = struct((edges // Q * DT, Q), F32)
    wide = struct((DT, width), F32)
    slots = (block_counts, in_index, out_index, triplet_cos, w_bilinear)

    down, slope = call(
        down_kernel, (table, struct((DT, edges), F32)), (edge_embed, w_down), 3
    )
    source = {4: down}
    source[3] = shift(down, "gy", 1)
    source[5] = shift(down, "gy", -1)
    source[1] = shift(down, "gx", 1)
    source[7] = shift(down, "gx", -1)
    source[0] = shift(source[3], "gx", 1)
    source[2] = shift(source[5], "gx", 1)
    source[6] = shift(source[3], "gx", -1)
    source[8] = shift(source[5], "gx", -1)

    feats = {}
    trip = None
    for pairs in ((4,), (3, 5, 1, 7), (0, 2, 6, 8)):
        n = len(pairs)
        base = trip is not None
        args = slots + tuple(source[k] for k in pairs) + ((trip,) if base else ())
        trip, feat = call(
            functools.partial(forward_kernel, pairs, base),
            (stack, struct((n * DT, SLOTS), BF16)),
            args,
            n,
            smem=(0,),
        )
        for i, k in enumerate(pairs):
            feats[k] = feat[i * DT : (i + 1) * DT]

    steps = edges // Q
    updated, d_trip, grad_up = pl.pallas_call(
        middle_kernel,
        grid=(steps,),
        out_shape=(struct((edges, width), BF16), table, wide),
        in_specs=[
            pl.BlockSpec((Q, width), lambda r: (r, 0)),
            pl.BlockSpec((Q, width), lambda r: (r, 0)),
            pl.BlockSpec((DT, Q), lambda r: (r, 0)),
            pl.BlockSpec((DT, width), lambda r: (0, 0)),
        ],
        out_specs=(
            pl.BlockSpec((Q, width), lambda r: (r, 0)),
            pl.BlockSpec((DT, Q), lambda r: (0, r)),
            pl.BlockSpec((DT, width), lambda r: (0, 0)),
        ),
        compiler_params=pltpu.CompilerParams(vmem_limit_bytes=VMEM_LIMIT),
        cost_estimate=pl.CostEstimate(
            flops=5_000_000_000, bytes_accessed=15_000_000, transcendentals=0
        ),
    )(edge_embed, cotangent, trip, w_up)

    d_source = {}
    grad_bil = None
    for pairs in ((0, 1, 2), (6, 7, 8), (3, 4, 5)):
        n = len(pairs)
        base = grad_bil is not None
        args = slots + (d_trip,) + tuple(feats[k] for k in pairs) + ((grad_bil,) if base else ())
        out, grad_bil = call(
            functools.partial(backward_kernel, pairs, base),
            (struct((n, DT, edges), BF16), wide),
            args,
            n,
            smem=(0,),
        )
        d_source[pairs[0] // 3] = out
    before = shift(d_source[2], "gx", 1)
    after = shift(d_source[0], "gx", -1)
    rows = d_source[1].astype(F32) + before.astype(F32) + after.astype(F32)
    below = shift(rows[2].astype(BF16), "gy", 1)
    above = shift(rows[0].astype(BF16), "gy", -1)

    d_pre, grad_down = call(
        final_kernel, (table, wide), (edge_embed, slope, rows[1], below, above), 3
    )
    grad_embed = pl.pallas_call(
        embed_kernel,
        grid=(steps,),
        out_shape=struct((edges, width), BF16),
        in_specs=[
            pl.BlockSpec((Q, width), lambda r: (r, 0)),
            pl.BlockSpec((DT, Q), lambda r: (0, r)),
            pl.BlockSpec((width, DT), lambda r: (0, 0)),
        ],
        out_specs=pl.BlockSpec((Q, width), lambda r: (r, 0)),
        compiler_params=pltpu.CompilerParams(vmem_limit_bytes=VMEM_LIMIT),
        cost_estimate=pl.CostEstimate(
            flops=3_000_000_000, bytes_accessed=9_000_000, transcendentals=0
        ),
    )(cotangent, d_pre, w_down)

    early = all_sum(jnp.concatenate([grad_bil, grad_up], axis=0))
    late = all_sum(grad_down)
    scale = float(edges * lax.axis_size("gx") * lax.axis_size("gy")) ** (-0.5)
    grad_down, grad_bil, grad_up = call(
        functools.partial(finish_kernel, scale),
        (struct((width, DT), F32), struct((L * DT, DT), F32), wide),
        (late, early[:DT], early[DT:]),
        2,
    )
    return (updated, grad_embed, grad_down, grad_bil, grad_up)


def solution(mesh):
    both = P(("gx", "gy"), None)
    in_specs = (both, both, P(), P(), P(), both, both, both, both)
    out_specs = (both, both, P(), P(), P())
    return jax.shard_map(shards, mesh=mesh, in_specs=in_specs, out_specs=out_specs, check_vma=False)
```

```python
import functools

import jax
import jax.numpy as jnp
from jax import lax
from jax.experimental import pallas as pl
from jax.experimental.pallas import tpu as pltpu
from jax.sharding import PartitionSpec as P

L = 8
DT = 64
TB = 64
SLOTS = 768
PAIR_US = 0.4
Q = 256
F32 = jnp.float32
BF16 = jnp.bfloat16
VMEM_LIMIT = 8 * 2**20

NN = (((1,), (0,)), ((), ()))
NT = (((1,), (1,)), ((), ()))
TN = (((0,), (0,)), ((), ()))


def dot(a, b, dims):
    return lax.dot_general(a, b, dims, preferred_element_type=F32)


def sigmoid(value):
    return 0.5 * jnp.tanh(0.5 * value) + 0.5


def legendre(cosine):
    terms = [jnp.ones_like(cosine), cosine]
    for order in range(1, L - 1):
        terms.append(
            ((2 * order + 1) * cosine * terms[order] - order * terms[order - 1])
            * (1.0 / (order + 1))
        )
    return terms


def slot_kernel(
    ks_ref, counts_ref, in_ref, out_ref, cos_ref, in_to, out_to, valid_to, basis_to, core_to
):
    core_to[...] = jnp.full(core_to.shape, ks_ref[in_to.shape[0]], jnp.int32)
    lane = lax.broadcasted_iota(jnp.int32, (1, 2 * TB), 1)
    rows = []
    for p in range(in_to.shape[0]):
        k = ks_ref[p]
        in_to[p : p + 1, :] = in_ref[pl.ds(k, 1), :]
        out_to[p : p + 1, :] = out_ref[pl.ds(k, 1), :]
        rows.append(cos_ref[pl.ds(k, 1), :])
        for t in range(SLOTS // (2 * TB)):
            count = jnp.where(lane < TB, counts_ref[k, 2 * t], counts_ref[k, 2 * t + 1])
            valid_to[p : p + 1, t * 2 * TB : (t + 1) * 2 * TB] = (
                (lane & (TB - 1)) < count
            ).astype(F32)
    for l, term in enumerate(legendre(jnp.concatenate(rows, axis=0))):
        basis_to[l] = term


def one_hot(index):
    low = (index & (Q - 1)).astype(F32).astype(BF16)
    row = lax.broadcasted_iota(jnp.int32, (Q, 128), 0).astype(F32).astype(BF16)
    row = jnp.concatenate([row] * (SLOTS // 128), axis=1)
    return jnp.where(row == low, jnp.ones((), BF16), jnp.zeros((), BF16))


def stacked(table):
    parts = table.shape[1] // Q
    return jnp.concatenate([table[:, r * Q : (r + 1) * Q] for r in range(parts)], axis=0)


def pick(table, hot, high):
    parts = table.shape[1] // Q
    found = dot(stacked(table), hot, NN)
    total = found[:DT]
    for r in range(1, parts):
        total = jnp.where(high == r, found[r * DT : (r + 1) * DT], total)
    return total


def collect(values, hot, high, parts):
    low = values.astype(BF16)
    zero = jnp.zeros((), BF16)
    rows = [jnp.where(high == r, low, zero) for r in range(parts)]
    return dot(jnp.concatenate(rows, axis=0), hot, NT)


def expand(basis_ref, p, values):
    return jnp.concatenate(
        [(basis_ref[l, p : p + 1, :] * values).astype(BF16) for l in range(L)], axis=0
    )


def down_kernel(edge_ref, w_ref, down_ref, slope_ref):
    pre = dot(w_ref[...], edge_ref[...], NT)
    sig = sigmoid(pre)
    down_ref[...] = (pre * sig).astype(BF16)
    slope_ref[...] = sig * (1.0 + pre * (1.0 - sig))


def forward_kernel(places, base, rows, in_ref, out_ref, valid_ref, basis_ref, w_ref, *refs):
    n = len(places)
    sources = refs[:n]
    total_ref = refs[n] if base else None
    outs = refs[n + base :]
    trip_ref, feat_ref = outs[:2]
    w = w_ref[...]
    if rows:
        outs[2][...] = jnp.concatenate(
            [w[:, l * DT : (l + 1) * DT].astype(F32).T for l in range(L)], axis=1
        ).astype(BF16)
    parts = sources[0].shape[-1] // Q
    for i, p in enumerate(places):
        in_idx = in_ref[p : p + 1, :]
        out_idx = out_ref[p : p + 1, :]
        feat = pick(sources[i][...], one_hot(in_idx), in_idx // Q)
        feat_ref[i * DT : (i + 1) * DT, :] = feat.astype(BF16)
        message = dot(w, expand(basis_ref, p, feat), NN) * valid_ref[p : p + 1, :]
        part = collect(message, one_hot(out_idx), out_idx // Q, parts)
        if i == 0:
            trip_ref[...] = part + total_ref[...] if base else part
        else:
            trip_ref[...] += part


def middle_kernel(scale, cot_ref, trip_ref, w_ref, d_trip_ref, grad_ref, trip_b_ref):
    w = w_ref[...]
    for r in range(cot_ref.shape[0] // Q):
        trip = trip_ref[r * DT : (r + 1) * DT, :].astype(BF16)
        trip_b_ref[r * DT : (r + 1) * DT, :] = trip
        up_act = dot(trip, w, TN)
        sig = sigmoid(up_act)
        slope = sig * (1.0 + up_act * (1.0 - sig))
        d_act = (cot_ref[r * Q : (r + 1) * Q, :].astype(F32) * slope).astype(BF16)
        d_trip_ref[:, r * Q : (r + 1) * Q] = dot(w, d_act, NT).astype(BF16)
        part = dot(trip, d_act, NN) * scale
        grad_ref[...] = part if r == 0 else grad_ref[...] + part


def updated_kernel(after_ref, edge_ref, trip_ref, w_ref, updated_ref, token_ref):
    token_ref[...] = jnp.zeros_like(token_ref)
    rows = updated_ref.shape[0]
    base = pl.program_id(0) * rows
    for r in range(rows // Q):
        at = pl.multiple_of((base // Q + r) * DT, DT)
        up_act = dot(trip_ref[pl.ds(at, DT), :], w_ref[...], TN)
        edge = edge_ref[pl.ds(pl.multiple_of(base + r * Q, Q), Q), :].astype(F32)
        updated_ref[r * Q : (r + 1) * Q, :] = (edge + up_act * sigmoid(up_act)).astype(BF16)


def backward_kernel(
    places, base, scale, in_ref, out_ref, valid_ref, basis_ref, w_ref, d_trip_ref, *refs
):
    feat_refs = refs[: len(places)]
    grad_base = refs[len(places)] if base else None
    own_ref, pair_ref, grad_ref = refs[-3:]
    w_rows = w_ref[...]
    d_trip = d_trip_ref[...]
    parts = d_trip.shape[1] // Q
    total = grad_base[...] if base else None
    for i, p in enumerate(places):
        in_idx = in_ref[p : p + 1, :]
        out_idx = out_ref[p : p + 1, :]
        d_message = pick(d_trip, one_hot(out_idx), out_idx // Q) * valid_ref[p : p + 1, :]
        spread = expand(basis_ref, p, d_message)
        part = dot(feat_refs[i][...], spread, NT)
        total = part if total is None else total + part
        d_feat = dot(w_rows, spread, NN)
        d_source = collect(d_feat, one_hot(in_idx), in_idx // Q, parts).astype(BF16)
        for r in range(parts):
            at, piece = slice(r * Q, (r + 1) * Q), d_source[r * DT : (r + 1) * DT]
            if i == 0:
                own_ref[:, at] = piece
            else:
                pair_ref[i - 1, :, at] = piece
    if scale is None:
        grad_ref[...] = total
    else:
        total = total * scale
        for l in range(L):
            grad_ref[:, l * DT : (l + 1) * DT] = total[:, l * DT : (l + 1) * DT].T


def meet_kernel(own_ref, far_ref, near_ref, *out_refs):
    for i, out_ref in enumerate(out_refs):
        total = own_ref[i].astype(F32) + far_ref[i].astype(F32) + near_ref[i].astype(F32)
        out_ref[...] = total.astype(BF16)


def final_kernel(scale, after_ref, edge_ref, slope_ref, core_ref, bil_ref, up_ref, *refs):
    terms, (d_pre_ref, keep_ref, send_ref) = refs[:-3], refs[-3:]
    d_down = terms[0][...].astype(F32)
    for term in terms[1:]:
        d_down = d_down + term[...].astype(F32)
    d_pre = (d_down * slope_ref[...]).astype(BF16)
    d_pre_ref[...] = d_pre
    grad = dot(d_pre, edge_ref[...], NN) * scale
    even = core_ref[0:1, :] == 0
    half = DT // 2
    keep_ref[:half, :] = jnp.where(even, grad[:half], grad[half:])
    send_ref[:half, :] = jnp.where(even, grad[half:], grad[:half])
    bil, up = bil_ref[...], up_ref[...]
    keep_ref[half:, :] = jnp.where(even, bil, up)
    send_ref[half:, :] = jnp.where(even, up, bil)


def embed_kernel(after_ref, cot_ref, d_pre_ref, w_ref, grad_ref, token_ref):
    token_ref[...] = jnp.zeros_like(token_ref)
    rows = grad_ref.shape[0]
    base = pl.multiple_of(pl.program_id(0) * rows, rows)
    part = dot(d_pre_ref[:, pl.ds(base, rows)], w_ref[...], TN)
    grad_ref[...] = (cot_ref[pl.ds(base, rows), :].astype(F32) + part).astype(BF16)


def finish_kernel(core_ref, mine_ref, other_ref, down_ref, bil_ref, up_ref):
    even = core_ref[0:1, :] == 0
    half = DT // 2
    mine, other = mine_ref[...], other_ref[...]
    first, second = jnp.where(even, mine, other), jnp.where(even, other, mine)
    down_ref[:half, :] = first[:half]
    down_ref[half:, :] = second[:half]
    bil_ref[...] = first[half:]
    up_ref[...] = second[half:]


def cost(us):
    return pl.CostEstimate(
        flops=int(us * 1.0e9), bytes_accessed=int(us * 3.0e6), transcendentals=0
    )


VMEM = pl.BlockSpec(memory_space=pltpu.VMEM)


def call(kernel, outs, args, us, smem=(), after=None):
    scalar = pl.BlockSpec(memory_space=pltpu.SMEM)
    specs = [scalar if i in smem else VMEM for i in range(len(args))]
    return pl.pallas_call(
        kernel,
        out_shape=outs,
        in_specs=specs if after is None else [VMEM] + specs,
        out_specs=jax.tree.map(lambda _: VMEM, outs),
        compiler_params=pltpu.CompilerParams(vmem_limit_bytes=VMEM_LIMIT),
        cost_estimate=cost(us),
    )(*(() if after is None else (after,)), *args)


def tiled(kernel, steps, args, out, us, after, shape=(8, 128)):
    block = (out.shape[0] // steps, out.shape[1])
    return pl.pallas_call(
        kernel,
        grid=(steps,),
        out_shape=(out, jax.ShapeDtypeStruct(shape, F32)),
        in_specs=[VMEM] * (len(args) + 1),
        out_specs=(
            pl.BlockSpec(block, lambda r: (r, 0)),
            VMEM,
        ),
        compiler_params=pltpu.CompilerParams(vmem_limit_bytes=VMEM_LIMIT),
        cost_estimate=cost(us),
    )(after, *args)


def swap(x, axis, partner):
    return lax.ppermute(x, axis, [(i, partner(i)) for i in range(lax.axis_size(axis))])


def near(x, axis):
    return swap(x, axis, lambda i: i ^ 1)


def far(x, axis):
    n = lax.axis_size(axis)
    return swap(x, axis, lambda i: (i + 1) % n if i % 2 else (i - 1) % n)


SIDE = 4


def mirror(i, unit):
    return i + (SIDE - 1 - 2 * (i // unit % SIDE)) * unit


BOTH = ("gx", "gy")
SUM_STEPS = (
    (lambda i, j: (i ^ 2, j), lambda i, j: (i ^ 8, j), lambda i, j: (i ^ 10, j)),
    (
        lambda i, j: (mirror(i, 2), j),
        lambda i, j: (mirror(i, 8), j),
        lambda i, j: (mirror(mirror(i, 2), 8), j),
    ),
    (lambda i, j: (i, j ^ 1), lambda i, j: (i, j ^ 3), lambda i, j: (i, j ^ 2)),
    (lambda i, j: (i, 7 - j),),
)


def sum_step(x, *partners):
    nx, ny = (lax.axis_size(axis) for axis in BOTH)
    x = x.astype(BF16)
    got = []
    for partner in partners:
        pairs = []
        for i in range(nx):
            for j in range(ny):
                to = partner(i, j)
                pairs.append((i * ny + j, to[0] * ny + to[1]))
        got.append(lax.ppermute(x, BOTH, pairs).astype(F32))
    total = x.astype(F32) + got[0]
    return total + (got[1] + got[2]) if len(got) == 3 else total


def together(*values):
    return lax.optimization_barrier(values)


def shards(
    edge_embed, cotangent, w_down, w_bilinear, w_up, in_index, out_index, triplet_cos, block_counts
):
    edges, width = edge_embed.shape
    struct = jax.ShapeDtypeStruct
    table = struct((DT, edges), BF16)
    stack = struct((edges // Q * DT, Q), F32)
    wide = struct((DT, width), F32)
    scale = float(edges * lax.axis_size("gx") * lax.axis_size("gy")) ** (-0.5)
    steps = edges // Q
    row, whole = (lambda r: (r, 0)), (lambda r: (0, 0))
    column = lambda r: (0, r)
    w_down_t, w_bil_t = w_down.T, w_bilinear.T
    core = lax.rem(lax.axis_index("gx"), 2)

    near_a = 2 - 2 * core
    near_b = 2 - 2 * lax.rem(lax.axis_index("gy"), 2)
    far_a, far_b = 2 - near_a, 2 - near_b
    ks = [4, 3 + near_b, 3 + far_b, 3 * near_a + 1, 3 * far_a + 1]
    ks += [3 * a + b for a in (near_a, far_a) for b in (near_b, far_b)]
    ks = jnp.stack([jnp.asarray(k, jnp.int32) for k in ks + [core]])
    *slots, core = call(
        slot_kernel,
        (
            struct(in_index.shape, jnp.int32),
            struct(in_index.shape, jnp.int32),
            struct(in_index.shape, F32),
            struct((L,) + in_index.shape, F32),
            struct((8, width), jnp.int32),
        ),
        (ks, block_counts, in_index, out_index, triplet_cos),
        1,
        smem=(0, 1),
    )
    slots = tuple(slots)

    down, slope = call(
        down_kernel, (table, struct((DT, edges), F32)), (edge_embed, w_down_t), 1
    )
    source = {0: down, 1: near(down, "gy"), 2: far(down, "gy")}
    source[4], source[3] = far(down, "gx"), near(down, "gx")
    feats = {}
    trip = w_rows = None
    for places in ((0,), (3, 4), (1, 2), (5, 6), (7, 8)):
        if places == (1, 2):
            source[1], source[2], trip = together(source[1], source[2], trip)
            source[7], source[8] = far(source[1], "gx"), far(source[2], "gx")
            source[5], source[6] = near(source[1], "gx"), near(source[2], "gx")
        n = len(places)
        base = trip is not None
        args = slots + (w_bil_t,) + tuple(source[p] for p in places) + ((trip,) if base else ())
        outs = (stack, struct((n * DT, SLOTS), BF16))
        outs += () if base else (struct((DT, L * DT), BF16),)
        trip, feat, *rest = call(
            functools.partial(forward_kernel, places, base, not base),
            outs,
            args,
            n * PAIR_US,
        )
        w_rows = rest[0] if rest else w_rows
        for i, p in enumerate(places):
            feats[p] = feat[i * DT : (i + 1) * DT]

    d_trip, grad_up, trip = call(
        functools.partial(middle_kernel, scale),
        (table, wide, struct(stack.shape, BF16)),
        (cotangent, trip, w_up),
        2,
    )

    sent = []
    grad_bil = None
    for places in ((4, 7, 8), (3, 5, 6), (0, 1, 2)):
        n = len(places)
        base = grad_bil is not None
        args = slots + (w_rows, d_trip) + tuple(feats[p] for p in places)
        args += (grad_bil,) if base else ()
        last = scale if places[0] == 0 else None
        *out, grad_bil = call(
            functools.partial(backward_kernel, places, base, last),
            (table, struct((n - 1, DT, edges), BF16), wide),
            args,
            n * PAIR_US,
        )
        sent.append(out)
    far_pair, far_own = far(sent[0][1], "gx"), far(sent[0][0], "gx")
    near_own, near_pair = (near(x, "gx") for x in sent[1])
    own, pair = sent[2]
    to_near, to_far = call(meet_kernel, (table, table), (pair, far_pair, near_pair), 0.5)
    from_near, from_far = near(to_near, "gy"), far(to_far, "gy")
    result = struct((edges, width), BF16)
    updated, token = tiled(updated_kernel, 4, (edge_embed, trip, w_up), result, 2, after=to_near)
    share = struct((DT // 2 + DT, width), F32)
    d_pre, keep, send = call(
        functools.partial(final_kernel, scale),
        (table, share, share),
        (edge_embed, slope, core, grad_bil, grad_up)
        + (own, far_own, near_own, from_near, from_far),
        1,
        after=token,
    )
    sums = keep + near(send, "gx")
    sums = sum_step(sums, *SUM_STEPS[0])
    grad_embed, token = tiled(
        embed_kernel, 4, (cotangent, d_pre, w_down_t), result, 2, sums, sums.shape
    )
    sums = sum_step(sums, *SUM_STEPS[1]) + token
    for step in SUM_STEPS[2:]:
        sums = sum_step(sums, *step)
    grad_down, grad_bil, grad_up = call(
        finish_kernel,
        (wide, wide, wide),
        (core, sums, near(sums, "gx")),
        1,
    )
    return (updated, grad_embed, grad_down.T, grad_bil.T, grad_up)


def solution(mesh):
    both = P(("gx", "gy"), None)
    in_specs = (both, both, P(), P(), P(), both, both, both, both)
    out_specs = (both, both, P(), P(), P())
    return jax.shard_map(shards, mesh=mesh, in_specs=in_specs, out_specs=out_specs, check_vma=False)
```

```python
import functools

import jax
import jax.numpy as jnp
from jax import lax
from jax.experimental import pallas as pl
from jax.experimental.pallas import tpu as pltpu
from jax.sharding import PartitionSpec as P

L = 8
DT = 64
TB = 64
SLOTS = 768
FORWARD_US = 0.04
BACKWARD_US = 4
Q = 256
F32 = jnp.float32
BF16 = jnp.bfloat16
VMEM_LIMIT = 8 * 2**20

NN = (((1,), (0,)), ((), ()))
NT = (((1,), (1,)), ((), ()))
TN = (((0,), (0,)), ((), ()))


def dot(a, b, dims):
    return lax.dot_general(a, b, dims, preferred_element_type=F32)


def sigmoid(value):
    return 0.5 * jnp.tanh(0.5 * value) + 0.5


def legendre(cosine):
    terms = [jnp.ones_like(cosine), cosine]
    for order in range(1, L - 1):
        terms.append(
            ((2 * order + 1) * cosine * terms[order] - order * terms[order - 1])
            * (1.0 / (order + 1))
        )
    return terms


def slot_kernel(ks_ref, counts_ref, in_ref, out_ref, cos_ref, down_ref, *refs):
    in_to, out_to, valid_to, basis_to, core_to, down_to = refs
    down_to[...] = down_ref[...]
    core_to[...] = jnp.full(core_to.shape, ks_ref[in_to.shape[0]], jnp.int32)
    lane = lax.broadcasted_iota(jnp.int32, (1, 2 * TB), 1)
    rows = []
    for p in range(in_to.shape[0]):
        k = ks_ref[p]
        in_to[p : p + 1, :] = in_ref[pl.ds(k, 1), :]
        out_to[p : p + 1, :] = out_ref[pl.ds(k, 1), :]
        rows.append(cos_ref[pl.ds(k, 1), :])
        for t in range(SLOTS // (2 * TB)):
            count = jnp.where(lane < TB, counts_ref[k, 2 * t], counts_ref[k, 2 * t + 1])
            valid_to[p : p + 1, t * 2 * TB : (t + 1) * 2 * TB] = (
                (lane & (TB - 1)) < count
            ).astype(F32)
    for l, term in enumerate(legendre(jnp.concatenate(rows, axis=0))):
        basis_to[l] = term


def one_hot(index):
    low = (index & (Q - 1)).astype(F32).astype(BF16)
    row = lax.broadcasted_iota(jnp.int32, (Q, 128), 0).astype(F32).astype(BF16)
    row = jnp.concatenate([row] * (SLOTS // 128), axis=1)
    return jnp.where(row == low, jnp.ones((), BF16), jnp.zeros((), BF16))


def stacked(table):
    parts = table.shape[1] // Q
    return jnp.concatenate([table[:, r * Q : (r + 1) * Q] for r in range(parts)], axis=0)


def pick(table, hot, high):
    parts = table.shape[1] // Q
    found = dot(stacked(table), hot, NN)
    total = found[:DT]
    for r in range(1, parts):
        total = jnp.where(high == r, found[r * DT : (r + 1) * DT], total)
    return total


def collect(values, hot, high, parts):
    low = values.astype(BF16)
    zero = jnp.zeros((), BF16)
    rows = [jnp.where(high == r, low, zero) for r in range(parts)]
    return dot(jnp.concatenate(rows, axis=0), hot, NT)


def expand(basis_ref, p, values):
    return jnp.concatenate(
        [(basis_ref[l, p : p + 1, :] * values).astype(BF16) for l in range(L)], axis=0
    )


def down_kernel(edge_ref, w_ref, down_ref, slope_ref):
    pre = dot(w_ref[...], edge_ref[...], NT)
    sig = sigmoid(pre)
    down_ref[...] = (pre * sig).astype(BF16)
    slope_ref[...] = sig * (1.0 + pre * (1.0 - sig))


def forward_kernel(places, base, rows, in_ref, out_ref, valid_ref, basis_ref, w_ref, *refs):
    sources, refs = refs[: len(places)], refs[len(places) :]
    total_ref, outs = refs[0] if base else None, refs[base:]
    trip_ref, feat_ref = outs[:2]
    w = w_ref[...]
    if rows:
        outs[2][...] = jnp.concatenate(
            [w[:, l * DT : (l + 1) * DT].astype(F32).T for l in range(L)], axis=1
        ).astype(BF16)
    parts = sources[0].shape[-1] // Q
    for i, p in enumerate(places):
        in_idx = in_ref[p : p + 1, :]
        out_idx = out_ref[p : p + 1, :]
        feat = pick(sources[i][...], one_hot(in_idx), in_idx // Q)
        feat_ref[i * DT : (i + 1) * DT, :] = feat.astype(BF16)
        message = dot(w, expand(basis_ref, p, feat), NN) * valid_ref[p : p + 1, :]
        part = collect(message, one_hot(out_idx), out_idx // Q, parts)
        if i == 0:
            trip_ref[...] = part + total_ref[...] if base else part
        else:
            trip_ref[...] += part


def middle_kernel(scale, cot_ref, trip_ref, w_ref, d_trip_ref, grad_ref, trip_b_ref):
    w = w_ref[...]
    for r in range(cot_ref.shape[0] // Q):
        trip = trip_ref[r * DT : (r + 1) * DT, :].astype(BF16)
        trip_b_ref[r * DT : (r + 1) * DT, :] = trip
        up_act = dot(trip, w, TN)
        sig = sigmoid(up_act)
        slope = sig * (1.0 + up_act * (1.0 - sig))
        d_act = (cot_ref[r * Q : (r + 1) * Q, :].astype(F32) * slope).astype(BF16)
        d_trip_ref[:, r * Q : (r + 1) * Q] = dot(w, d_act, NT).astype(BF16)
        part = dot(trip, d_act, NN) * scale
        grad_ref[...] = part if r == 0 else grad_ref[...] + part


def updated_kernel(after_ref, edge_ref, trip_ref, w_ref, updated_ref, token_ref):
    token_ref[...] = jnp.zeros_like(token_ref)
    rows = updated_ref.shape[0]
    base = pl.program_id(0) * rows
    for r in range(rows // Q):
        at = pl.multiple_of((base // Q + r) * DT, DT)
        up_act = dot(trip_ref[pl.ds(at, DT), :], w_ref[...], TN)
        edge = edge_ref[pl.ds(pl.multiple_of(base + r * Q, Q), Q), :].astype(F32)
        updated_ref[r * Q : (r + 1) * Q, :] = (edge + up_act * sigmoid(up_act)).astype(BF16)


def backward_kernel(
    places, base, scale, in_ref, out_ref, valid_ref, basis_ref, w_ref, d_trip_ref, *refs
):
    feat_refs = refs[: len(places)]
    grad_base = refs[len(places)] if base else None
    outs, grad_ref = refs[len(places) + base : -1], refs[-1]
    w_rows = w_ref[...]
    d_trip = d_trip_ref[...]
    parts = d_trip.shape[1] // Q
    total = grad_base[...] if base else None
    for i, p in enumerate(places):
        in_idx = in_ref[p : p + 1, :]
        out_idx = out_ref[p : p + 1, :]
        d_message = pick(d_trip, one_hot(out_idx), out_idx // Q) * valid_ref[p : p + 1, :]
        spread = expand(basis_ref, p, d_message)
        part = dot(feat_refs[i][...], spread, NT)
        total = part if total is None else total + part
        d_feat = dot(w_rows, spread, NN)
        d_source = collect(d_feat, one_hot(in_idx), in_idx // Q, parts).astype(BF16)
        for r in range(parts):
            at, piece = slice(r * Q, (r + 1) * Q), d_source[r * DT : (r + 1) * DT]
            if len(outs) == 1:
                outs[0][i, :, at] = piece
            elif i == 0:
                outs[0][:, at] = piece
            else:
                outs[1][i - 1, :, at] = piece
    if scale is None:
        grad_ref[...] = total
    else:
        total = total * scale
        for l in range(L):
            grad_ref[:, l * DT : (l + 1) * DT] = total[:, l * DT : (l + 1) * DT].T


def meet_kernel(own_ref, pair_ref, far_pair_ref, near_ref, far_own_ref, *refs):
    *pair_to, own_to, far_own_to = refs
    for i, out_ref in enumerate(pair_to):
        total = pair_ref[i].astype(F32) + near_ref[i + 1].astype(F32)
        out_ref[...] = (total + far_pair_ref[i].astype(F32)).astype(BF16)
    own_to[...] = (own_ref[...].astype(F32) + near_ref[0].astype(F32)).astype(BF16)
    far_own_to[...] = far_own_ref[...]


def final_kernel(scale, after_ref, edge_ref, slope_ref, core_ref, bil_ref, up_ref, *refs):
    terms, (d_pre_ref, keep_ref, send_ref) = refs[:-3], refs[-3:]
    d_down = terms[0][...].astype(F32)
    for term in terms[1:]:
        d_down = d_down + term[...].astype(F32)
    d_pre = (d_down * slope_ref[...]).astype(BF16)
    d_pre_ref[...] = d_pre
    grad = dot(d_pre, edge_ref[...], NN) * scale
    even = core_ref[0:1, :] == 0
    half = DT // 2
    keep_ref[:half, :] = jnp.where(even, grad[:half], grad[half:])
    send_ref[:half, :] = jnp.where(even, grad[half:], grad[:half])
    bil, up = bil_ref[...], up_ref[...]
    keep_ref[half:, :] = jnp.where(even, bil, up)
    send_ref[half:, :] = jnp.where(even, up, bil)


def embed_kernel(after_ref, cot_ref, d_pre_ref, w_ref, grad_ref, token_ref):
    token_ref[...] = jnp.zeros_like(token_ref)
    rows = grad_ref.shape[0]
    base = pl.multiple_of(pl.program_id(0) * rows, rows)
    part = dot(d_pre_ref[:, pl.ds(base, rows)], w_ref[...], TN)
    grad_ref[...] = (cot_ref[pl.ds(base, rows), :].astype(F32) + part).astype(BF16)


def finish_kernel(core_ref, mine_ref, other_ref, down_ref, bil_ref, up_ref):
    even = core_ref[0:1, :] == 0
    half = DT // 2
    mine, other = mine_ref[...], other_ref[...]
    first, second = jnp.where(even, mine, other), jnp.where(even, other, mine)
    down_ref[:half, :] = first[:half]
    down_ref[half:, :] = second[:half]
    bil_ref[...] = first[half:]
    up_ref[...] = second[half:]


def cost(us):
    return pl.CostEstimate(
        flops=int(us * 1.0e9), bytes_accessed=int(us * 3.0e6), transcendentals=0
    )


VMEM = pl.BlockSpec(memory_space=pltpu.VMEM)


def call(kernel, outs, args, us, smem=(), after=None):
    scalar = pl.BlockSpec(memory_space=pltpu.SMEM)
    specs = [scalar if i in smem else VMEM for i in range(len(args))]
    return pl.pallas_call(
        kernel,
        out_shape=outs,
        in_specs=specs if after is None else [VMEM] + specs,
        out_specs=jax.tree.map(lambda _: VMEM, outs),
        compiler_params=pltpu.CompilerParams(vmem_limit_bytes=VMEM_LIMIT),
        cost_estimate=cost(us),
    )(*(() if after is None else (after,)), *args)


def tiled(kernel, steps, args, out, us, after, shape=(8, 128)):
    block = (out.shape[0] // steps, out.shape[1])
    return pl.pallas_call(
        kernel,
        grid=(steps,),
        out_shape=(out, jax.ShapeDtypeStruct(shape, F32)),
        in_specs=[VMEM] * (len(args) + 1),
        out_specs=(
            pl.BlockSpec(block, lambda r: (r, 0)),
            VMEM,
        ),
        compiler_params=pltpu.CompilerParams(vmem_limit_bytes=VMEM_LIMIT),
        cost_estimate=cost(us),
    )(after, *args)


def swap(x, axis, partner):
    return lax.ppermute(x, axis, [(i, partner(i)) for i in range(lax.axis_size(axis))])


def near(x, axis):
    return swap(x, axis, lambda i: i ^ 1)


def far(x, axis):
    n = lax.axis_size(axis)
    return swap(x, axis, lambda i: (i + 1) % n if i % 2 else (i - 1) % n)


SIDE = 4


def mirror(i, unit):
    return i + (SIDE - 1 - 2 * (i // unit % SIDE)) * unit


BOTH = ("gx", "gy")
SUM_STEPS = (
    (lambda i, j: (i ^ 2, j), lambda i, j: (i ^ 8, j), lambda i, j: (i ^ 10, j)),
    (
        lambda i, j: (mirror(i, 2), j),
        lambda i, j: (mirror(i, 8), j),
        lambda i, j: (mirror(mirror(i, 2), 8), j),
    ),
    (lambda i, j: (i, j ^ 1), lambda i, j: (i, j ^ 3), lambda i, j: (i, j ^ 2)),
    (lambda i, j: (i, 7 - j),),
)


def sum_step(x, *partners):
    nx, ny = (lax.axis_size(axis) for axis in BOTH)
    x = x.astype(BF16)
    got = []
    for partner in partners:
        pairs = []
        for i in range(nx):
            for j in range(ny):
                to = partner(i, j)
                pairs.append((i * ny + j, to[0] * ny + to[1]))
        got.append(lax.ppermute(x, BOTH, pairs).astype(F32))
    total = x.astype(F32) + got[0]
    return total + (got[1] + got[2]) if len(got) == 3 else total


def shards(
    edge_embed, cotangent, w_down, w_bilinear, w_up, in_index, out_index, triplet_cos, block_counts
):
    edges, width = edge_embed.shape
    struct = jax.ShapeDtypeStruct
    table = struct((DT, edges), BF16)
    stack = struct((edges // Q * DT, Q), F32)
    wide = struct((DT, width), F32)
    scale = float(edges * lax.axis_size("gx") * lax.axis_size("gy")) ** (-0.5)
    steps = edges // Q
    row, whole = (lambda r: (r, 0)), (lambda r: (0, 0))
    column = lambda r: (0, r)
    w_down_t, w_bil_t = w_down.T, w_bilinear.T
    core = lax.rem(lax.axis_index("gx"), 2)

    near_a = 2 - 2 * core
    near_b = 2 - 2 * lax.rem(lax.axis_index("gy"), 2)
    far_a, far_b = 2 - near_a, 2 - near_b
    ks = [4, 3 + near_b, 3 + far_b, 3 * near_a + 1, 3 * far_a + 1]
    ks += [3 * a + b for a in (near_a, far_a) for b in (near_b, far_b)]
    ks = jnp.stack([jnp.asarray(k, jnp.int32) for k in ks + [core]])
    down, slope = call(
        down_kernel,
        (table, struct((DT, edges), F32)),
        (edge_embed, w_down_t),
        1,
    )
    *slots, core, down_later = call(
        slot_kernel,
        (
            struct(in_index.shape, jnp.int32),
            struct(in_index.shape, jnp.int32),
            struct(in_index.shape, F32),
            struct((L,) + in_index.shape, F32),
            struct((8, width), jnp.int32),
            table,
        ),
        (ks, block_counts, in_index, out_index, triplet_cos, down),
        0.1,
        smem=(0, 1),
    )
    slots = tuple(slots)

    source = {0: down, 1: near(down, "gy"), 2: far(down, "gy")}
    source[4], source[3] = far(down_later, "gx"), near(down_later, "gx")
    source[7], source[8] = far(source[1], "gx"), far(source[4], "gy")
    source[5], source[6] = near(source[1], "gx"), near(source[2], "gx")
    feats = {}
    trip = w_rows = None
    for places in ((0, 3, 4), (1, 2, 5, 6), (7, 8)):
        n = len(places)
        base = trip is not None
        args = slots + (w_bil_t,) + tuple(source[p] for p in places) + ((trip,) if base else ())
        outs = (stack, struct((n * DT, SLOTS), BF16))
        outs += () if base else (struct((DT, L * DT), BF16),)
        trip, feat, *rest = call(
            functools.partial(forward_kernel, places, base, not base),
            outs,
            args,
            n * FORWARD_US,
        )
        w_rows = rest[0] if rest else w_rows
        for i, p in enumerate(places):
            feats[p] = feat[i * DT : (i + 1) * DT]

    d_trip, grad_up, trip = call(
        functools.partial(middle_kernel, scale),
        (table, wide, struct(stack.shape, BF16)),
        (cotangent, trip, w_up),
        2,
    )

    sent = []
    grad_bil = None
    for places in ((7, 8), (4, 3, 5, 6), (0, 1, 2)):
        n = len(places)
        base = grad_bil is not None
        args = slots + (w_rows, d_trip) + tuple(feats[p] for p in places)
        args += (grad_bil,) if base else ()
        last = scale if places[0] == 0 else None
        *out, grad_bil = call(
            functools.partial(backward_kernel, places, base, last),
            (struct((n, DT, edges), BF16), wide)
            if places[0] == 7
            else (table, struct((n - 1, DT, edges), BF16), wide),
            args,
            n * BACKWARD_US,
        )
        sent.append(out)
    (far_pair,), (far_own, near_all), (own, pair) = sent
    far_pair, near_all = far(far_pair, "gx"), near(near_all, "gx")
    to_near, to_far, own, far_own = call(
        meet_kernel, (table,) * 4, (own, pair, far_pair, near_all, far_own), 0.5
    )
    from_near, from_far = near(to_near, "gy"), far(to_far, "gy")
    far_own = far(far_own, "gx")
    result = struct((edges, width), BF16)
    updated, token = tiled(updated_kernel, 4, (edge_embed, trip, w_up), result, 2, after=to_near)
    share = struct((DT // 2 + DT, width), F32)
    d_pre, keep, send = call(
        functools.partial(final_kernel, scale),
        (table, share, share),
        (edge_embed, slope, core, grad_bil, grad_up)
        + (own, far_own, from_near, from_far),
        1,
        after=token,
    )
    sums = keep + near(send, "gx")
    for step in SUM_STEPS[:2]:
        sums = sum_step(sums, *step)
    grad_embed, token = tiled(
        embed_kernel, 4, (cotangent, d_pre, w_down_t), result, 2, sums, sums.shape
    )
    sums = sum_step(sums, *SUM_STEPS[2]) + token
    sums = sum_step(sums, *SUM_STEPS[3])
    grad_down, grad_bil, grad_up = call(
        finish_kernel,
        (wide, wide, wide),
        (core, sums, near(sums, "gx")),
        1,
    )
    return (updated, grad_embed, grad_down.T, grad_bil.T, grad_up)


def solution(mesh):
    both = P(("gx", "gy"), None)
    in_specs = (both, both, P(), P(), P(), both, both, both, both)
    out_specs = (both, both, P(), P(), P())
    return jax.shard_map(shards, mesh=mesh, in_specs=in_specs, out_specs=out_specs, check_vma=False)
```

```python
import functools

import jax
import jax.numpy as jnp
from jax import lax
from jax.experimental import pallas as pl
from jax.experimental.pallas import tpu as pltpu
from jax.sharding import PartitionSpec as P

L = 8
DT = 64
TB = 64
SLOTS = 768
FORWARD_US = 0.04
BACKWARD_US = 4
Q = 256
F32 = jnp.float32
BF16 = jnp.bfloat16
VMEM_LIMIT = 8 * 2**20

NN = (((1,), (0,)), ((), ()))
NT = (((1,), (1,)), ((), ()))
TN = (((0,), (0,)), ((), ()))


def dot(a, b, dims):
    return lax.dot_general(a, b, dims, preferred_element_type=F32)


def sigmoid(value):
    return 0.5 * jnp.tanh(0.5 * value) + 0.5


def legendre(cosine):
    terms = [jnp.ones_like(cosine), cosine]
    for order in range(1, L - 1):
        terms.append(
            ((2 * order + 1) * cosine * terms[order] - order * terms[order - 1])
            * (1.0 / (order + 1))
        )
    return terms


def slot_kernel(ks_ref, counts_ref, in_ref, out_ref, cos_ref, down_ref, *refs):
    in_to, out_to, valid_to, basis_to, core_to, down_to = refs
    down_to[...] = down_ref[...]
    core_to[...] = jnp.full(core_to.shape, ks_ref[in_to.shape[0]], jnp.int32)
    lane = lax.broadcasted_iota(jnp.int32, (1, 2 * TB), 1)
    rows = []
    for p in range(in_to.shape[0]):
        k = ks_ref[p]
        in_to[p : p + 1, :] = in_ref[pl.ds(k, 1), :]
        out_to[p : p + 1, :] = out_ref[pl.ds(k, 1), :]
        rows.append(cos_ref[pl.ds(k, 1), :])
        for t in range(SLOTS // (2 * TB)):
            count = jnp.where(lane < TB, counts_ref[k, 2 * t], counts_ref[k, 2 * t + 1])
            valid_to[p : p + 1, t * 2 * TB : (t + 1) * 2 * TB] = (
                (lane & (TB - 1)) < count
            ).astype(F32)
    for l, term in enumerate(legendre(jnp.concatenate(rows, axis=0))):
        basis_to[l] = term


def one_hot(index):
    low = (index & (Q - 1)).astype(F32).astype(BF16)
    row = lax.broadcasted_iota(jnp.int32, (Q, 128), 0).astype(F32).astype(BF16)
    row = jnp.concatenate([row] * (SLOTS // 128), axis=1)
    return jnp.where(row == low, jnp.ones((), BF16), jnp.zeros((), BF16))


def stacked(table):
    parts = table.shape[1] // Q
    return jnp.concatenate([table[:, r * Q : (r + 1) * Q] for r in range(parts)], axis=0)


def pick(table, hot, high):
    parts = table.shape[1] // Q
    found = dot(stacked(table), hot, NN)
    total = found[:DT]
    for r in range(1, parts):
        total = jnp.where(high == r, found[r * DT : (r + 1) * DT], total)
    return total


def collect(values, hot, high, parts):
    low = values.astype(BF16)
    zero = jnp.zeros((), BF16)
    rows = [jnp.where(high == r, low, zero) for r in range(parts)]
    return dot(jnp.concatenate(rows, axis=0), hot, NT)


def expand(basis_ref, p, values):
    return jnp.concatenate(
        [(basis_ref[l, p : p + 1, :] * values).astype(BF16) for l in range(L)], axis=0
    )


def down_kernel(edge_ref, w_ref, down_ref, slope_ref):
    pre = dot(w_ref[...], edge_ref[...], NT)
    sig = sigmoid(pre)
    down_ref[...] = (pre * sig).astype(BF16)
    slope_ref[...] = sig * (1.0 + pre * (1.0 - sig))


def forward_kernel(places, base, rows, split, in_ref, out_ref, valid_ref, basis_ref, w_ref, *refs):
    sources, refs = refs[: len(places)], refs[len(places) :]
    if split:
        whole, rest = sources[0][...], sources[1][...]
        sources = whole[:DT], jnp.concatenate([whole[DT:], rest], axis=0)
    total_ref, outs = refs[0] if base else None, refs[base:]
    trip_ref, feat_ref = outs[:2]
    w = w_ref[...]
    if rows:
        outs[3][...] = sources[0][...]
        outs[2][...] = jnp.concatenate(
            [w[:, l * DT : (l + 1) * DT].astype(F32).T for l in range(L)], axis=1
        ).astype(BF16)
    parts = trip_ref.shape[0] // DT
    for i, p in enumerate(places):
        in_idx = in_ref[p : p + 1, :]
        out_idx = out_ref[p : p + 1, :]
        source = sources[i] if split else sources[i][...]
        feat = pick(source, one_hot(in_idx), in_idx // Q)
        feat_ref[i * DT : (i + 1) * DT, :] = feat.astype(BF16)
        message = dot(w, expand(basis_ref, p, feat), NN) * valid_ref[p : p + 1, :]
        part = collect(message, one_hot(out_idx), out_idx // Q, parts)
        if i == 0:
            trip_ref[...] = part + total_ref[...] if base else part
        else:
            trip_ref[...] += part


def middle_kernel(scale, cot_ref, trip_ref, w_ref, d_trip_ref, grad_ref, trip_b_ref):
    w = w_ref[...]
    for r in range(cot_ref.shape[0] // Q):
        trip = trip_ref[r * DT : (r + 1) * DT, :].astype(BF16)
        trip_b_ref[r * DT : (r + 1) * DT, :] = trip
        up_act = dot(trip, w, TN)
        sig = sigmoid(up_act)
        slope = sig * (1.0 + up_act * (1.0 - sig))
        d_act = (cot_ref[r * Q : (r + 1) * Q, :].astype(F32) * slope).astype(BF16)
        d_trip_ref[:, r * Q : (r + 1) * Q] = dot(w, d_act, NT).astype(BF16)
        part = dot(trip, d_act, NN) * scale
        grad_ref[...] = part if r == 0 else grad_ref[...] + part


def updated_kernel(after_ref, edge_ref, trip_ref, w_ref, updated_ref, token_ref):
    token_ref[...] = jnp.zeros_like(token_ref)
    rows = updated_ref.shape[0]
    base = pl.program_id(0) * rows
    for r in range(rows // Q):
        at = pl.multiple_of((base // Q + r) * DT, DT)
        up_act = dot(trip_ref[pl.ds(at, DT), :], w_ref[...], TN)
        edge = edge_ref[pl.ds(pl.multiple_of(base + r * Q, Q), Q), :].astype(F32)
        updated_ref[r * Q : (r + 1) * Q, :] = (edge + up_act * sigmoid(up_act)).astype(BF16)


def backward_kernel(
    places, base, scale, in_ref, out_ref, valid_ref, basis_ref, w_ref, d_trip_ref, *refs
):
    feat_refs = refs[: len(places)]
    grad_base = refs[len(places)] if base else None
    outs, grad_ref = refs[len(places) + base : -1], refs[-1]
    w_rows = w_ref[...]
    d_trip = d_trip_ref[...]
    parts = d_trip.shape[1] // Q
    total = grad_base[...] if base else None
    for i, p in enumerate(places):
        in_idx = in_ref[p : p + 1, :]
        out_idx = out_ref[p : p + 1, :]
        d_message = pick(d_trip, one_hot(out_idx), out_idx // Q) * valid_ref[p : p + 1, :]
        spread = expand(basis_ref, p, d_message)
        part = dot(feat_refs[i][...], spread, NT)
        total = part if total is None else total + part
        d_feat = dot(w_rows, spread, NN)
        d_source = collect(d_feat, one_hot(in_idx), in_idx // Q, parts).astype(BF16)
        for r in range(parts):
            at, piece = slice(r * Q, (r + 1) * Q), d_source[r * DT : (r + 1) * DT]
            if len(outs) == 1:
                outs[0][i, :, at] = piece
            elif i == 0:
                outs[0][:, at] = piece
            else:
                outs[1][i - 1, :, at] = piece
    if scale is None:
        grad_ref[...] = total
    else:
        total = total * scale
        for l in range(L):
            grad_ref[:, l * DT : (l + 1) * DT] = total[:, l * DT : (l + 1) * DT].T


def meet_kernel(own_ref, pair_ref, far_pair_ref, near_ref, far_own_ref, *refs):
    *pair_to, own_to, far_own_to = refs
    for i, out_ref in enumerate(pair_to):
        total = pair_ref[i].astype(F32) + near_ref[i + 1].astype(F32)
        out_ref[...] = (total + far_pair_ref[i].astype(F32)).astype(BF16)
    own_to[...] = (own_ref[...].astype(F32) + near_ref[0].astype(F32)).astype(BF16)
    far_own_to[...] = far_own_ref[...]


def final_kernel(scale, after_ref, edge_ref, slope_ref, core_ref, bil_ref, up_ref, *refs):
    terms, (d_pre_ref, keep_ref, send_ref) = refs[:-3], refs[-3:]
    d_down = terms[0][...].astype(F32)
    for term in terms[1:]:
        d_down = d_down + term[...].astype(F32)
    d_pre = (d_down * slope_ref[...]).astype(BF16)
    d_pre_ref[...] = d_pre
    grad = dot(d_pre, edge_ref[...], NN) * scale
    even = core_ref[0:1, :] == 0
    half = DT // 2
    keep_ref[:half, :] = jnp.where(even, grad[:half], grad[half:])
    send_ref[:half, :] = jnp.where(even, grad[half:], grad[:half])
    bil, up = bil_ref[...], up_ref[...]
    keep_ref[half:, :] = jnp.where(even, bil, up)
    send_ref[half:, :] = jnp.where(even, up, bil)


def embed_kernel(after_ref, cot_ref, d_pre_ref, w_ref, grad_ref, token_ref):
    token_ref[...] = jnp.zeros_like(token_ref)
    rows = grad_ref.shape[0]
    base = pl.multiple_of(pl.program_id(0) * rows, rows)
    part = dot(d_pre_ref[:, pl.ds(base, rows)], w_ref[...], TN)
    grad_ref[...] = (cot_ref[pl.ds(base, rows), :].astype(F32) + part).astype(BF16)


def finish_kernel(core_ref, mine_ref, other_ref, down_ref, bil_ref, up_ref):
    even = core_ref[0:1, :] == 0
    half = DT // 2
    mine, other = mine_ref[...], other_ref[...]
    first, second = jnp.where(even, mine, other), jnp.where(even, other, mine)
    down_ref[:half, :] = first[:half]
    down_ref[half:, :] = second[:half]
    bil_ref[...] = first[half:]
    up_ref[...] = second[half:]


def cost(us):
    return pl.CostEstimate(
        flops=int(us * 1.0e9), bytes_accessed=int(us * 3.0e6), transcendentals=0
    )


VMEM = pl.BlockSpec(memory_space=pltpu.VMEM)


def call(kernel, outs, args, us, smem=(), after=None):
    scalar = pl.BlockSpec(memory_space=pltpu.SMEM)
    specs = [scalar if i in smem else VMEM for i in range(len(args))]
    return pl.pallas_call(
        kernel,
        out_shape=outs,
        in_specs=specs if after is None else [VMEM] + specs,
        out_specs=jax.tree.map(lambda _: VMEM, outs),
        compiler_params=pltpu.CompilerParams(vmem_limit_bytes=VMEM_LIMIT),
        cost_estimate=cost(us),
    )(*(() if after is None else (after,)), *args)


def tiled(kernel, steps, args, out, us, after, shape=(8, 128)):
    block = (out.shape[0] // steps, out.shape[1])
    return pl.pallas_call(
        kernel,
        grid=(steps,),
        out_shape=(out, jax.ShapeDtypeStruct(shape, F32)),
        in_specs=[VMEM] * (len(args) + 1),
        out_specs=(
            pl.BlockSpec(block, lambda r: (r, 0)),
            VMEM,
        ),
        compiler_params=pltpu.CompilerParams(vmem_limit_bytes=VMEM_LIMIT),
        cost_estimate=cost(us),
    )(after, *args)


def swap(x, axis, partner):
    return lax.ppermute(x, axis, [(i, partner(i)) for i in range(lax.axis_size(axis))])


def near(x, axis):
    return swap(x, axis, lambda i: i ^ 1)


def far(x, axis):
    n = lax.axis_size(axis)
    return swap(x, axis, lambda i: (i + 1) % n if i % 2 else (i - 1) % n)


SIDE = 4


def mirror(i, unit):
    return i + (SIDE - 1 - 2 * (i // unit % SIDE)) * unit


BOTH = ("gx", "gy")
SUM_STEPS = (
    (lambda i, j: (i ^ 2, j), lambda i, j: (i ^ 8, j), lambda i, j: (i ^ 10, j)),
    (
        lambda i, j: (mirror(i, 2), j),
        lambda i, j: (mirror(i, 8), j),
        lambda i, j: (mirror(mirror(i, 2), 8), j),
    ),
    (lambda i, j: (i, j ^ 1), lambda i, j: (i, j ^ 3), lambda i, j: (i, j ^ 2)),
    (lambda i, j: (i, 7 - j),),
)


def sum_step(x, *partners):
    nx, ny = (lax.axis_size(axis) for axis in BOTH)
    x = x.astype(BF16)
    got = []
    for partner in partners:
        pairs = []
        for i in range(nx):
            for j in range(ny):
                to = partner(i, j)
                pairs.append((i * ny + j, to[0] * ny + to[1]))
        got.append(lax.ppermute(x, BOTH, pairs).astype(F32))
    total = x.astype(F32) + got[0]
    return total + (got[1] + got[2]) if len(got) == 3 else total


def shards(
    edge_embed, cotangent, w_down, w_bilinear, w_up, in_index, out_index, triplet_cos, block_counts
):
    edges, width = edge_embed.shape
    struct = jax.ShapeDtypeStruct
    table = struct((DT, edges), BF16)
    stack = struct((edges // Q * DT, Q), F32)
    wide = struct((DT, width), F32)
    scale = float(edges * lax.axis_size("gx") * lax.axis_size("gy")) ** (-0.5)
    steps = edges // Q
    row, whole = (lambda r: (r, 0)), (lambda r: (0, 0))
    column = lambda r: (0, r)
    w_down_t, w_bil_t = w_down.T, w_bilinear.T
    core = lax.rem(lax.axis_index("gx"), 2)

    near_a = 2 - 2 * core
    near_b = 2 - 2 * lax.rem(lax.axis_index("gy"), 2)
    far_a, far_b = 2 - near_a, 2 - near_b
    ks = [4, 3 + near_b, 3 + far_b, 3 * near_a + 1, 3 * far_a + 1]
    ks += [3 * a + b for a in (near_a, far_a) for b in (near_b, far_b)]
    ks = jnp.stack([jnp.asarray(k, jnp.int32) for k in ks + [core]])
    down, slope = call(
        down_kernel,
        (table, struct((DT, edges), F32)),
        (edge_embed, w_down_t),
        1,
    )
    *slots, core, down_later = call(
        slot_kernel,
        (
            struct(in_index.shape, jnp.int32),
            struct(in_index.shape, jnp.int32),
            struct(in_index.shape, F32),
            struct((L,) + in_index.shape, F32),
            struct((8, width), jnp.int32),
            table,
        ),
        (ks, block_counts, in_index, out_index, triplet_cos, down),
        0.1,
        smem=(0, 1),
    )
    slots = tuple(slots)

    source = {0: down, 1: near(down, "gy"), 2: far(down, "gy")}
    feats = {}
    trip = w_rows = None
    for places in ((0,), (3, 4), (1, 2, 5, 6), (7, 8)):
        n = len(places)
        base = trip is not None
        split = places == (7, 8)
        blocks = (along_x, along_y) if split else tuple(source[p] for p in places)
        args = slots + (w_bil_t,) + blocks + ((trip,) if base else ())
        outs = (stack, struct((n * DT, SLOTS), BF16))
        outs += () if base else (struct((DT, L * DT), BF16), table)
        trip, feat, *rest = call(
            functools.partial(forward_kernel, places, base, not base, split),
            outs,
            args,
            n * FORWARD_US,
        )
        if rest:
            w_rows, down = rest
            source[4], source[3] = far(down, "gx"), near(down, "gx")
            half = DT // 2
            along_x = far(jnp.concatenate([source[1], source[2][:half]], axis=0), "gx")
            along_y = far(source[4][half:], "gy")
            source[5], source[6] = near(source[1], "gx"), near(source[2], "gx")
        for i, p in enumerate(places):
            feats[p] = feat[i * DT : (i + 1) * DT]

    d_trip, grad_up, trip = call(
        functools.partial(middle_kernel, scale),
        (table, wide, struct(stack.shape, BF16)),
        (cotangent, trip, w_up),
        2,
    )

    sent = []
    grad_bil = None
    for places in ((7, 8), (4, 3, 5, 6), (0, 1, 2)):
        n = len(places)
        base = grad_bil is not None
        args = slots + (w_rows, d_trip) + tuple(feats[p] for p in places)
        args += (grad_bil,) if base else ()
        last = scale if places[0] == 0 else None
        *out, grad_bil = call(
            functools.partial(backward_kernel, places, base, last),
            (struct((n, DT, edges), BF16), wide)
            if places[0] == 7
            else (table, struct((n - 1, DT, edges), BF16), wide),
            args,
            n * BACKWARD_US,
        )
        sent.append(out)
    (far_pair,), (far_own, near_all), (own, pair) = sent
    far_pair, near_all = far(far_pair, "gx"), near(near_all, "gx")
    to_near, to_far, own, far_own = call(
        meet_kernel, (table,) * 4, (own, pair, far_pair, near_all, far_own), 0.5
    )
    from_near, from_far = near(to_near, "gy"), far(to_far, "gy")
    far_own = far(far_own, "gx")
    result = struct((edges, width), BF16)
    updated, token = tiled(updated_kernel, 4, (edge_embed, trip, w_up), result, 2, after=to_near)
    share = struct((DT // 2 + DT, width), F32)
    d_pre, keep, send = call(
        functools.partial(final_kernel, scale),
        (table, share, share),
        (edge_embed, slope, core, grad_bil, grad_up)
        + (own, far_own, from_near, from_far),
        1,
        after=token,
    )
    sums = keep + near(send, "gx")
    for step in SUM_STEPS[:2]:
        sums = sum_step(sums, *step)
    grad_embed, token = tiled(
        embed_kernel, 4, (cotangent, d_pre, w_down_t), result, 2, sums, sums.shape
    )
    sums = sum_step(sums, *SUM_STEPS[2]) + token
    sums = sum_step(sums, *SUM_STEPS[3])
    grad_down, grad_bil, grad_up = call(
        finish_kernel,
        (wide, wide, wide),
        (core, sums, near(sums, "gx")),
        1,
    )
    return (updated, grad_embed, grad_down.T, grad_bil.T, grad_up)


def solution(mesh):
    both = P(("gx", "gy"), None)
    in_specs = (both, both, P(), P(), P(), both, both, both, both)
    out_specs = (both, both, P(), P(), P())
    return jax.shard_map(shards, mesh=mesh, in_specs=in_specs, out_specs=out_specs, check_vma=False)
```

```python
import functools

import jax
import jax.numpy as jnp
from jax import lax
from jax.experimental import pallas as pl
from jax.experimental.pallas import tpu as pltpu
from jax.sharding import PartitionSpec as P

L = 8
DT = 64
TB = 64
SLOTS = 768
FORWARD_US = 0.04
BACKWARD_US = 4
Q = 256
F32 = jnp.float32
BF16 = jnp.bfloat16
VMEM_LIMIT = 8 * 2**20

NN = (((1,), (0,)), ((), ()))
NT = (((1,), (1,)), ((), ()))
TN = (((0,), (0,)), ((), ()))


def dot(a, b, dims):
    return lax.dot_general(a, b, dims, preferred_element_type=F32)


def sigmoid(value):
    return 0.5 * jnp.tanh(0.5 * value) + 0.5


def legendre(cosine):
    terms = [jnp.ones_like(cosine), cosine]
    for order in range(1, L - 1):
        terms.append(
            ((2 * order + 1) * cosine * terms[order] - order * terms[order - 1])
            * (1.0 / (order + 1))
        )
    return terms


def slot_kernel(ks_ref, counts_ref, in_ref, out_ref, cos_ref, down_ref, *refs):
    in_to, out_to, valid_to, basis_to, core_to, down_to = refs
    down_to[...] = down_ref[...]
    core_to[...] = jnp.full(core_to.shape, ks_ref[in_to.shape[0]], jnp.int32)
    lane = lax.broadcasted_iota(jnp.int32, (1, 2 * TB), 1)
    rows = []
    for p in range(in_to.shape[0]):
        k = ks_ref[p]
        in_to[p : p + 1, :] = in_ref[pl.ds(k, 1), :]
        out_to[p : p + 1, :] = out_ref[pl.ds(k, 1), :]
        rows.append(cos_ref[pl.ds(k, 1), :])
        for t in range(SLOTS // (2 * TB)):
            count = jnp.where(lane < TB, counts_ref[k, 2 * t], counts_ref[k, 2 * t + 1])
            valid_to[p : p + 1, t * 2 * TB : (t + 1) * 2 * TB] = (
                (lane & (TB - 1)) < count
            ).astype(F32)
    for l, term in enumerate(legendre(jnp.concatenate(rows, axis=0))):
        basis_to[l] = term


def one_hot(index):
    low = (index & (Q - 1)).astype(F32).astype(BF16)
    row = lax.broadcasted_iota(jnp.int32, (Q, 128), 0).astype(F32).astype(BF16)
    row = jnp.concatenate([row] * (SLOTS // 128), axis=1)
    return jnp.where(row == low, jnp.ones((), BF16), jnp.zeros((), BF16))


def stacked(table):
    parts = table.shape[1] // Q
    return jnp.concatenate([table[:, r * Q : (r + 1) * Q] for r in range(parts)], axis=0)


def pick(table, hot, high):
    parts = table.shape[1] // Q
    found = dot(stacked(table), hot, NN)
    total = found[:DT]
    for r in range(1, parts):
        total = jnp.where(high == r, found[r * DT : (r + 1) * DT], total)
    return total


def collect(values, hot, high, parts):
    low = values.astype(BF16)
    zero = jnp.zeros((), BF16)
    rows = [jnp.where(high == r, low, zero) for r in range(parts)]
    return dot(jnp.concatenate(rows, axis=0), hot, NT)


def expand(basis_ref, p, values):
    return jnp.concatenate(
        [(basis_ref[l, p : p + 1, :] * values).astype(BF16) for l in range(L)], axis=0
    )


def down_kernel(edge_ref, w_ref, down_ref, slope_ref):
    pre = dot(w_ref[...], edge_ref[...], NT)
    sig = sigmoid(pre)
    down_ref[...] = (pre * sig).astype(BF16)
    slope_ref[...] = sig * (1.0 + pre * (1.0 - sig))


def forward_kernel(places, base, rows, split, in_ref, out_ref, valid_ref, basis_ref, w_ref, *refs):
    sources, refs = refs[: len(places)], refs[len(places) :]
    if split:
        whole, rest = sources[0][...], sources[1][...]
        sources = whole[:DT], jnp.concatenate([whole[DT:], rest], axis=0)
    total_ref, outs = refs[0] if base else None, refs[base:]
    trip_ref, feat_ref = outs[:2]
    w = w_ref[...]
    if rows:
        outs[3][...] = sources[0][...]
        outs[2][...] = jnp.concatenate(
            [w[:, l * DT : (l + 1) * DT].astype(F32).T for l in range(L)], axis=1
        ).astype(BF16)
    parts = trip_ref.shape[0] // DT
    for i, p in enumerate(places):
        in_idx = in_ref[p : p + 1, :]
        out_idx = out_ref[p : p + 1, :]
        source = sources[i] if split else sources[i][...]
        feat = pick(source, one_hot(in_idx), in_idx // Q)
        feat_ref[i * DT : (i + 1) * DT, :] = feat.astype(BF16)
        message = dot(w, expand(basis_ref, p, feat), NN) * valid_ref[p : p + 1, :]
        part = collect(message, one_hot(out_idx), out_idx // Q, parts)
        if i == 0:
            trip_ref[...] = part + total_ref[...] if base else part
        else:
            trip_ref[...] += part


def middle_kernel(scale, cot_ref, trip_ref, w_ref, d_trip_ref, grad_ref, trip_b_ref):
    w = w_ref[...]
    for r in range(cot_ref.shape[0] // Q):
        trip = trip_ref[r * DT : (r + 1) * DT, :].astype(BF16)
        trip_b_ref[r * DT : (r + 1) * DT, :] = trip
        up_act = dot(trip, w, TN)
        sig = sigmoid(up_act)
        slope = sig * (1.0 + up_act * (1.0 - sig))
        d_act = (cot_ref[r * Q : (r + 1) * Q, :].astype(F32) * slope).astype(BF16)
        d_trip_ref[:, r * Q : (r + 1) * Q] = dot(w, d_act, NT).astype(BF16)
        part = dot(trip, d_act, NN) * scale
        grad_ref[...] = part if r == 0 else grad_ref[...] + part


def updated_kernel(after_ref, edge_ref, trip_ref, w_ref, updated_ref, token_ref):
    token_ref[...] = jnp.zeros_like(token_ref)
    rows = updated_ref.shape[0]
    base = pl.program_id(0) * rows
    for r in range(rows // Q):
        at = pl.multiple_of((base // Q + r) * DT, DT)
        up_act = dot(trip_ref[pl.ds(at, DT), :], w_ref[...], TN)
        edge = edge_ref[pl.ds(pl.multiple_of(base + r * Q, Q), Q), :].astype(F32)
        updated_ref[r * Q : (r + 1) * Q, :] = (edge + up_act * sigmoid(up_act)).astype(BF16)


def backward_kernel(
    places, base, scale, in_ref, out_ref, valid_ref, basis_ref, w_ref, d_trip_ref, *refs
):
    feat_refs = refs[: len(places)]
    grad_base = refs[len(places)] if base else None
    outs, grad_ref = refs[len(places) + base : -1], refs[-1]
    w_rows = w_ref[...]
    d_trip = d_trip_ref[...]
    parts = d_trip.shape[1] // Q
    total = grad_base[...] if base else None
    for i, p in enumerate(places):
        in_idx = in_ref[p : p + 1, :]
        out_idx = out_ref[p : p + 1, :]
        d_message = pick(d_trip, one_hot(out_idx), out_idx // Q) * valid_ref[p : p + 1, :]
        spread = expand(basis_ref, p, d_message)
        part = dot(feat_refs[i][...], spread, NT)
        total = part if total is None else total + part
        d_feat = dot(w_rows, spread, NN)
        d_source = collect(d_feat, one_hot(in_idx), in_idx // Q, parts).astype(BF16)
        for r in range(parts):
            at, piece = slice(r * Q, (r + 1) * Q), d_source[r * DT : (r + 1) * DT]
            if len(outs) == 1:
                outs[0][i, :, at] = piece
            elif i == 0:
                outs[0][:, at] = piece
            else:
                outs[1][i - 1, :, at] = piece
    if scale is None:
        grad_ref[...] = total
    else:
        total = total * scale
        for l in range(L):
            grad_ref[:, l * DT : (l + 1) * DT] = total[:, l * DT : (l + 1) * DT].T


def meet_kernel(own_ref, pair_ref, far_pair_ref, near_ref, far_own_ref, *refs):
    *pair_to, own_to, far_own_to = refs
    for i, out_ref in enumerate(pair_to):
        total = pair_ref[i].astype(F32) + near_ref[i + 1].astype(F32)
        out_ref[...] = (total + far_pair_ref[i].astype(F32)).astype(BF16)
    own_to[...] = (own_ref[...].astype(F32) + near_ref[0].astype(F32)).astype(BF16)
    far_own_to[...] = far_own_ref[...]


def final_kernel(scale, after_ref, edge_ref, slope_ref, core_ref, bil_ref, up_ref, *refs):
    terms, (d_pre_ref, keep_ref, send_ref) = refs[:-3], refs[-3:]
    d_down = terms[0][...].astype(F32)
    for term in terms[1:]:
        d_down = d_down + term[...].astype(F32)
    d_pre = (d_down * slope_ref[...]).astype(BF16)
    d_pre_ref[...] = d_pre
    grad = dot(d_pre, edge_ref[...], NN) * scale
    even = core_ref[0:1, :] == 0
    half = DT // 2
    keep_ref[:half, :] = jnp.where(even, grad[:half], grad[half:])
    send_ref[:half, :] = jnp.where(even, grad[half:], grad[:half])
    bil, up = bil_ref[...], up_ref[...]
    keep_ref[half:, :] = jnp.where(even, bil, up)
    send_ref[half:, :] = jnp.where(even, up, bil)


def embed_kernel(after_ref, cot_ref, d_pre_ref, w_ref, grad_ref, token_ref):
    token_ref[...] = jnp.zeros_like(token_ref)
    rows = grad_ref.shape[0]
    base = pl.multiple_of(pl.program_id(0) * rows, rows)
    part = dot(d_pre_ref[:, pl.ds(base, rows)], w_ref[...], TN)
    grad_ref[...] = (cot_ref[pl.ds(base, rows), :].astype(F32) + part).astype(BF16)


def finish_kernel(core_ref, mine_ref, other_ref, down_ref, bil_ref, up_ref):
    even = core_ref[0:1, :] == 0
    half = DT // 2
    mine, other = mine_ref[...], other_ref[...]
    first, second = jnp.where(even, mine, other), jnp.where(even, other, mine)
    down_ref[:half, :] = first[:half]
    down_ref[half:, :] = second[:half]
    bil_ref[...] = first[half:]
    up_ref[...] = second[half:]


def cost(us):
    return pl.CostEstimate(
        flops=int(us * 1.0e9), bytes_accessed=int(us * 3.0e6), transcendentals=0
    )


VMEM = pl.BlockSpec(memory_space=pltpu.VMEM)


def call(kernel, outs, args, us, smem=(), after=None):
    scalar = pl.BlockSpec(memory_space=pltpu.SMEM)
    specs = [scalar if i in smem else VMEM for i in range(len(args))]
    return pl.pallas_call(
        kernel,
        out_shape=outs,
        in_specs=specs if after is None else [VMEM] + specs,
        out_specs=jax.tree.map(lambda _: VMEM, outs),
        compiler_params=pltpu.CompilerParams(vmem_limit_bytes=VMEM_LIMIT),
        cost_estimate=cost(us),
    )(*(() if after is None else (after,)), *args)


def tiled(kernel, steps, args, out, us, after, shape=(8, 128)):
    block = (out.shape[0] // steps, out.shape[1])
    return pl.pallas_call(
        kernel,
        grid=(steps,),
        out_shape=(out, jax.ShapeDtypeStruct(shape, F32)),
        in_specs=[VMEM] * (len(args) + 1),
        out_specs=(
            pl.BlockSpec(block, lambda r: (r, 0)),
            VMEM,
        ),
        compiler_params=pltpu.CompilerParams(vmem_limit_bytes=VMEM_LIMIT),
        cost_estimate=cost(us),
    )(after, *args)


def swap(x, axis, partner):
    return lax.ppermute(x, axis, [(i, partner(i)) for i in range(lax.axis_size(axis))])


def near(x, axis):
    return swap(x, axis, lambda i: i ^ 1)


def far(x, axis):
    n = lax.axis_size(axis)
    return swap(x, axis, lambda i: (i + 1) % n if i % 2 else (i - 1) % n)


SIDE = 4


def mirror(i, unit):
    return i + (SIDE - 1 - 2 * (i // unit % SIDE)) * unit


BOTH = ("gx", "gy")
SUM_STEPS = (
    (lambda i, j: (i ^ 2, j), lambda i, j: (i ^ 8, j), lambda i, j: (i ^ 10, j)),
    (
        lambda i, j: (mirror(i, 2), j),
        lambda i, j: (mirror(i, 8), j),
        lambda i, j: (mirror(mirror(i, 2), 8), j),
    ),
    (lambda i, j: (i, j ^ 1), lambda i, j: (i, j ^ 3), lambda i, j: (i, j ^ 2)),
    (lambda i, j: (i, 7 - j),),
)


def sum_step(x, *partners):
    nx, ny = (lax.axis_size(axis) for axis in BOTH)
    x = x.astype(BF16)
    got = []
    for partner in partners:
        pairs = []
        for i in range(nx):
            for j in range(ny):
                to = partner(i, j)
                pairs.append((i * ny + j, to[0] * ny + to[1]))
        got.append(lax.ppermute(x, BOTH, pairs).astype(F32))
    total = x.astype(F32) + got[0]
    return total + (got[1] + got[2]) if len(got) == 3 else total


def shards(
    edge_embed, cotangent, w_down, w_bilinear, w_up, in_index, out_index, triplet_cos, block_counts
):
    edges, width = edge_embed.shape
    struct = jax.ShapeDtypeStruct
    table = struct((DT, edges), BF16)
    stack = struct((edges // Q * DT, Q), F32)
    wide = struct((DT, width), F32)
    scale = float(edges * lax.axis_size("gx") * lax.axis_size("gy")) ** (-0.5)
    steps = edges // Q
    row, whole = (lambda r: (r, 0)), (lambda r: (0, 0))
    column = lambda r: (0, r)
    w_down_t, w_bil_t = w_down.T, w_bilinear.T
    core = lax.rem(lax.axis_index("gx"), 2)

    near_a = 2 - 2 * core
    near_b = 2 - 2 * lax.rem(lax.axis_index("gy"), 2)
    far_a, far_b = 2 - near_a, 2 - near_b
    ks = [4, 3 + near_b, 3 + far_b, 3 * near_a + 1, 3 * far_a + 1]
    ks += [3 * a + b for a in (near_a, far_a) for b in (near_b, far_b)]
    ks = jnp.stack([jnp.asarray(k, jnp.int32) for k in ks + [core]])
    down, slope = call(
        down_kernel,
        (table, struct((DT, edges), F32)),
        (edge_embed, w_down_t),
        1,
    )
    *slots, core, down_later = call(
        slot_kernel,
        (
            struct(in_index.shape, jnp.int32),
            struct(in_index.shape, jnp.int32),
            struct(in_index.shape, F32),
            struct((L,) + in_index.shape, F32),
            struct((8, width), jnp.int32),
            table,
        ),
        (ks, block_counts, in_index, out_index, triplet_cos, down),
        0.1,
        smem=(0, 1),
    )
    slots = tuple(slots)

    source = {0: down, 1: near(down, "gy"), 2: far(down, "gy")}
    feats = {}
    trip = w_rows = None
    for places in ((0,), (3, 4, 1, 2, 5, 6), (7, 8)):
        n = len(places)
        base = trip is not None
        split = places == (7, 8)
        blocks = (along_x, along_y) if split else tuple(source[p] for p in places)
        args = slots + (w_bil_t,) + blocks + ((trip,) if base else ())
        outs = (stack, struct((n * DT, SLOTS), BF16))
        outs += () if base else (struct((DT, L * DT), BF16), table)
        trip, feat, *rest = call(
            functools.partial(forward_kernel, places, base, not base, split),
            outs,
            args,
            n * FORWARD_US,
        )
        if rest:
            w_rows, down = rest
            source[4], source[3] = far(down, "gx"), near(down, "gx")
            half = DT // 2
            along_x = far(jnp.concatenate([source[1], source[2][:half]], axis=0), "gx")
            along_y = far(source[4][half:], "gy")
            source[5], source[6] = near(source[1], "gx"), near(source[2], "gx")
        for i, p in enumerate(places):
            feats[p] = feat[i * DT : (i + 1) * DT]

    d_trip, grad_up, trip = call(
        functools.partial(middle_kernel, scale),
        (table, wide, struct(stack.shape, BF16)),
        (cotangent, trip, w_up),
        2,
    )

    sent = []
    grad_bil = None
    for places in ((7, 8), (4, 3, 5, 6), (0, 1, 2)):
        n = len(places)
        base = grad_bil is not None
        args = slots + (w_rows, d_trip) + tuple(feats[p] for p in places)
        args += (grad_bil,) if base else ()
        last = scale if places[0] == 0 else None
        *out, grad_bil = call(
            functools.partial(backward_kernel, places, base, last),
            (struct((n, DT, edges), BF16), wide)
            if places[0] == 7
            else (table, struct((n - 1, DT, edges), BF16), wide),
            args,
            n * BACKWARD_US,
        )
        sent.append(out)
    (far_pair,), (far_own, near_all), (own, pair) = sent
    far_pair, near_all = far(far_pair, "gx"), near(near_all, "gx")
    to_near, to_far, own, far_own = call(
        meet_kernel, (table,) * 4, (own, pair, far_pair, near_all, far_own), 0.5
    )
    from_near, from_far = near(to_near, "gy"), far(to_far, "gy")
    far_own = far(far_own, "gx")
    result = struct((edges, width), BF16)
    updated, token = tiled(updated_kernel, 4, (edge_embed, trip, w_up), result, 2, after=to_near)
    share = struct((DT // 2 + DT, width), F32)
    d_pre, keep, send = call(
        functools.partial(final_kernel, scale),
        (table, share, share),
        (edge_embed, slope, core, grad_bil, grad_up)
        + (own, far_own, from_near, from_far),
        1,
        after=token,
    )
    sums = keep + near(send, "gx")
    for step in SUM_STEPS[:2]:
        sums = sum_step(sums, *step)
    grad_embed, token = tiled(
        embed_kernel, 4, (cotangent, d_pre, w_down_t), result, 2, sums, sums.shape
    )
    sums = sum_step(sums, *SUM_STEPS[2]) + token
    sums = sum_step(sums, *SUM_STEPS[3])
    grad_down, grad_bil, grad_up = call(
        finish_kernel,
        (wide, wide, wide),
        (core, sums, near(sums, "gx")),
        1,
    )
    return (updated, grad_embed, grad_down.T, grad_bil.T, grad_up)


def solution(mesh):
    both = P(("gx", "gy"), None)
    in_specs = (both, both, P(), P(), P(), both, both, both, both)
    out_specs = (both, both, P(), P(), P())
    return jax.shard_map(shards, mesh=mesh, in_specs=in_specs, out_specs=out_specs, check_vma=False)
```
